32 devices in a mesh: grp: 2 (over x), gx: 16 (over z, y, core).
Axes of the slice: x: 2, y: 2, z: 4, core: 2. Of those that a mesh axis runs over, the one named last changes fastest.
Arguments:
- probes: float32 [32, 32, 128, 256], P('grp', 'gx'), parts along dimension 0, may hold values from -6 to 6
- kappa: float32 [64, 128, 256], P(('grp', 'gx')), parts along dimension 0, may hold values from 0.04 to 1.45
- delta: float32 [64, 128, 256], P(('grp', 'gx')), parts along dimension 0, may hold values from 0.2 to 1
- sensor_cells: int32 [4096], P(('grp', 'gx')), parts along dimension 0, may hold values from 0 to 1048575, as said below
- sensor_weights: float32 [4096], P(('grp', 'gx')), parts along dimension 0, may hold values from 1 to 8
Outputs:
- diag_estimate: float32 [64, 128, 256], P(('grp', 'gx')), parts along dimension 0
- sensor_grad: float32 [4096], P(('grp', 'gx')), parts along dimension 0
The draws below stay inside these ranges and needn't reach their ends.
There are 2 independent parts, one for each index of `grp`. The reference program is written for one: setup_inputs(seed, part) draws one part's arguments, and reference() takes and returns one part's arrays. A program takes and returns all parts, laid end to end along the dimension named above; each array names one. Nothing has to cross between parts.
Inputs may be any that keep to these rules, and one draw needn't show every extreme that they name: `sensor_cells`: flat row-major indices into the grid. The entries of block k of 128 are distinct cells whose first coordinate lies in [k * 2, (k + 1) * 2); each block holds the first and last cell of its slab.
All inputs are finite; a program needn't handle non-finite values.
Results may differ from the reference program's by a relative error of at most 0.0001.
Values sent between devices are 32-bit elements; how exact they have to be, the bound alone decides.
A program may use at most 128 MiB of HBM per device.

```python
import math
import jax
import jax.numpy as jnp

CX = 2
NY = 128
NZ = 256
PROBES = 16
SENS_DEV = 128
NX = 32
SENSORS = 2048


def draw_kappa(key, part):
    key = jax.random.fold_in(key, 11)
    rough = jnp.exp(jax.random.uniform(key, (NX, NY, NZ), jnp.float32, math.log(0.05), math.log(0.15)))
    ramp = jnp.exp(math.log(3.0) * jnp.arange(NX, dtype=jnp.float32) / (NX - 1))
    return (rough * ramp[:, None, None]).astype(jnp.float32)


def draw_sensor_cells(key, part):
    key = jax.random.fold_in(key, 17)
    blocks = NX // CX
    cells = CX * NY * NZ
    keys = jax.random.split(key, blocks)
    picked = jax.vmap(lambda k: jax.random.permutation(k, cells - 2)[:SENS_DEV - 2] + 1)(keys)
    first = jnp.zeros((blocks, 1), jnp.int32)
    last = jnp.full((blocks, 1), cells - 1, jnp.int32)
    local = jnp.concatenate([first, last, picked.astype(jnp.int32)], axis=1)
    offset = (jnp.arange(blocks, dtype=jnp.int32) * cells)[:, None]
    return (local + offset).reshape(-1).astype(jnp.int32)


def shard_levels(rng, extent, cuts, least, top_value):
    loudness = 1.0
    for dim, blocks in cuts:
        draws = jax.random.uniform(jax.random.fold_in(jax.random.fold_in(rng, 6), dim), (blocks,), jnp.float32, least / len(cuts), top_value / len(cuts))
        loudness = loudness * jnp.repeat(jnp.exp(draws), extent[dim] // blocks).reshape((-1,) + (1,) * (len(extent) - 1 - dim))
    return loudness


def centred(key, dims, width, limit, cuts=(), kind=jnp.bfloat16):
    loudness = shard_levels(key, dims, cuts, -0.22, 0.18) if cuts else 1.0
    array = jax.random.normal(key, dims, jnp.float32) * width * loudness
    return jnp.minimum(jnp.maximum(array, -limit), limit).astype(kind)


def setup_inputs(seed: int = 0, part: int = 0) -> dict:
    splits = jax.random.split(jax.random.key(seed), 6)
    part_splits = jax.random.split(jax.random.fold_in(splits[5], part), 6)
    return {
        "probes": centred(part_splits[0], (PROBES, NX, NY, NZ), 1.0, 6.0, ((1, 16),), jnp.float32),
        "kappa": draw_kappa(jax.random.fold_in(jax.random.fold_in(splits[5], part), 71), part),
        "delta": jnp.clip(0.2 + 0.8 * jax.random.uniform(part_splits[2], (NX, NY, NZ), jnp.float32) ** shard_levels(part_splits[2], (NX, NY, NZ), ((0, 16),), -0.2, 0.2), 0.2, 1.0),
        "sensor_cells": draw_sensor_cells(jax.random.fold_in(jax.random.fold_in(splits[5], part), 71), part),
        "sensor_weights": jnp.clip(jnp.exp(math.log(8.0) - 2.0794415 * jax.random.uniform(part_splits[4], (SENSORS,), jnp.float32) ** shard_levels(part_splits[4], (SENSORS,), ((0, 16),), -0.2, 0.2)), 1.0, 8.0),
    }


def apply_k(vx, kx, dx):
    vp = jnp.pad(vx, ((0, 0), (0, 0), (1, 1), (1, 1)))
    kp = jnp.pad(kx, ((0, 0), (1, 1), (1, 1)))
    vc = vp[:, 1:-1, 1:-1, 1:-1]
    kc = kp[1:-1, 1:-1, 1:-1]
    near = [(vp[:, :-2, 1:-1, 1:-1], kp[:-2, 1:-1, 1:-1]), (vp[:, 2:, 1:-1, 1:-1], kp[2:, 1:-1, 1:-1]),
            (vp[:, 1:-1, :-2, 1:-1], kp[1:-1, :-2, 1:-1]), (vp[:, 1:-1, 2:, 1:-1], kp[1:-1, 2:, 1:-1]),
            (vp[:, 1:-1, 1:-1, :-2], kp[1:-1, 1:-1, :-2]), (vp[:, 1:-1, 1:-1, 2:], kp[1:-1, 1:-1, 2:])]
    total = dx * vc
    for vn, kn in near:
        total = total + 0.5 * (kc + kn) * (vc - vn)
    return total


def diag_k(kx, dx):
    kp = jnp.pad(kx, ((0, 0), (1, 1), (1, 1)))
    kc = kp[1:-1, 1:-1, 1:-1]
    total = dx
    for kn in [kp[:-2, 1:-1, 1:-1], kp[2:, 1:-1, 1:-1], kp[1:-1, :-2, 1:-1], kp[1:-1, 2:, 1:-1], kp[1:-1, 1:-1, :-2], kp[1:-1, 1:-1, 2:]]:
        total = total + 0.5 * (kc + kn)
    return total


def reference(probes, kappa, delta, sensor_cells, sensor_weights):
    kx = jnp.pad(kappa, ((1, 1), (0, 0), (0, 0)))
    obs = jnp.zeros((NX * NY * NZ,), jnp.float32).at[sensor_cells].add(sensor_weights).reshape(NX, NY, NZ)
    kdiag = diag_k(kx, delta)
    precond = 1.0 / (kdiag * kdiag + obs)

    def hess(v):
        inner = apply_k(jnp.pad(v, ((0, 0), (1, 1), (0, 0), (0, 0))), kx, delta)
        return apply_k(jnp.pad(inner, ((0, 0), (1, 1), (0, 0), (0, 0))), kx, delta) + obs * v

    source = probes.astype(jnp.float32)
    solution = jnp.zeros_like(source)
    resid = source
    precon_res = precond * resid
    gamma = jnp.sum(resid * precon_res, axis=(1, 2, 3))
    direction = precon_res
    for step in range(2):
        image = hess(direction)
        alpha = gamma / jnp.sum(direction * image, axis=(1, 2, 3))
        solution = solution + alpha[:, None, None, None] * direction
        resid = resid - alpha[:, None, None, None] * image
        if step == 0:
            precon_res = precond * resid
            gamma_new = jnp.sum(resid * precon_res, axis=(1, 2, 3))
            direction = precon_res + (gamma_new / gamma)[:, None, None, None] * direction
            gamma = gamma_new
    diag_estimate = 0.5 * jnp.mean(source * solution, axis=0)
    sensor_grad = diag_estimate.reshape(-1)[sensor_cells]
    return diag_estimate, sensor_grad
```

```python
import functools

import jax
import jax.numpy as jnp
from jax import lax
from jax.experimental import pallas as pl
from jax.experimental.pallas import tpu as pltpu
from jax.sharding import PartitionSpec as P

GROUP = 4
CHUNK = 32
HIGH = lax.Precision.HIGHEST


def body(ng, sems, probes, kappa, delta, cells, weights, out, grad,
         bp, uu, tt, ww, qq, kap, dlt, kd, pre, obs, cx, cym, cyp, czm, czp,
         sc, sw, part1, part2, sum1, sum2, acc, red1, red2, relay,
         send_sem, recv_sem, local_sem):
    share = probes.shape[0] // GROUP
    rows, ny, nz = kappa.shape
    deep = GROUP * rows
    me = lax.axis_index("gx")
    g = lax.div(me, GROUP)
    j = lax.rem(me, GROUP)
    mates = {1: j + 1 - 2 * lax.rem(j, 2), 2: lax.rem(j + 2, 4), 3: 3 - j}
    has_low = g > 0
    has_high = g < ng - 1
    counter = [0]

    def remote(src, dst, target):
        k = counter[0]
        counter[0] += 1
        return pltpu.make_async_remote_copy(
            src_ref=src, dst_ref=dst, send_sem=send_sem.at[k],
            recv_sem=recv_sem.at[k], device_id={"gx": target},
            device_id_type=pl.DeviceIdType.MESH)

    barrier = pltpu.get_barrier_semaphore()
    for k in mates:
        pl.semaphore_signal(barrier, inc=1, device_id={"gx": g * GROUP + mates[k]},
                            device_id_type=pl.DeviceIdType.MESH)
    column = [lax.rem(g + d, ng) * GROUP + j for d in range(1, ng)]
    for other in column:
        pl.semaphore_signal(barrier, inc=1, device_id={"gx": other},
                            device_id_type=pl.DeviceIdType.MESH)
    pl.semaphore_wait(barrier, 3 + ng - 1)

    def mate(k):
        return g * GROUP + mates[k]

    mine_k = kap.at[pl.ds(1 + rows * j, rows)]
    mine_d = dlt.at[pl.ds(rows * j, rows)]
    direct = {}
    for k in (2, 1):
        direct[k] = [remote(kappa, mine_k, mate(k)), remote(delta, mine_d, mate(k))]
        for c in direct[k]:
            c.start()
    listed = []
    for k in (2, 3, 1):
        listed += [remote(cells, sc.at[j], mate(k)), remote(weights, sw.at[j], mate(k))]
    for c in listed:
        c.start()
    swaps = []
    for p in range(share):
        group = []
        for k in (2, 3, 1):
            c = remote(probes.at[share * mates[k] + p],
                       bp.at[p, pl.ds(rows * j, rows)], mate(k))
            c.start()
            group.append(c)
        swaps.append(group)
    own = [
        pltpu.make_async_copy(kappa, mine_k, local_sem.at[0]),
        pltpu.make_async_copy(delta, mine_d, local_sem.at[1]),
        pltpu.make_async_copy(cells, sc.at[j], local_sem.at[2]),
        pltpu.make_async_copy(weights, sw.at[j], local_sem.at[3]),
    ] + [
        pltpu.make_async_copy(probes.at[share * j + p],
                              bp.at[p, pl.ds(rows * j, rows)], local_sem.at[4 + p])
        for p in range(share)
    ]
    for c in own:
        c.start()

    class Halo:
        def __init__(self, low, first, last, high):
            self.up = remote(last, low, me + GROUP)
            self.down = remote(first, high, me - GROUP)

        def start(self):
            pl.when(has_high)(self.up.start)
            pl.when(has_low)(self.down.start)

        def wait_recv(self):
            pl.when(has_low)(self.up.wait_recv)
            pl.when(has_high)(self.down.wait_recv)

        def wait_send(self):
            pl.when(has_high)(self.up.wait_send)
            pl.when(has_low)(self.down.wait_send)

    def halo_of(field, p):
        f = field.at[p]
        return Halo(f.at[0], f.at[1], f.at[deep], f.at[deep + 1])

    zero = jnp.zeros((ny, nz), jnp.float32)

    @pl.when(g == 0)
    def _():
        kap[0] = zero
        for p in range(share):
            uu[p, 0] = zero
            tt[p, 0] = zero
            ww[p, 0] = zero

    @pl.when(g == ng - 1)
    def _():
        kap[deep + 1] = zero
        for p in range(share):
            uu[p, deep + 1] = zero
            tt[p, deep + 1] = zero
            ww[p, deep + 1] = zero

    for c in direct[2]:
        c.wait_recv()
    far_k = kap.at[pl.ds(1 + rows * mates[2], rows)]
    far_d = dlt.at[pl.ds(rows * mates[2], rows)]
    passed = [remote(far_k, far_k, mate(1)), remote(far_d, far_d, mate(1))]
    for c in passed:
        c.start()
    for c in listed:
        c.wait_recv()
    for c in own[:4]:
        c.wait()
    for k in range(GROUP):
        local = sc[k] - (g * GROUP + k) * (rows * ny * nz)
        row = lax.div(local, nz)
        col = local - row * nz
        sens = local.shape[1]
        at_row = lax.broadcasted_iota(jnp.int32, (rows * ny, sens), 0) == row
        at_col = lax.broadcasted_iota(jnp.int32, (nz, sens), 0) == col
        left = jnp.where(at_row, sw[k], 0.0)
        right = jnp.where(at_col, 1.0, 0.0)
        obs[rows * k:rows * (k + 1)] = lax.dot_general(
            left, right, (((1,), (1,)), ((), ())), precision=HIGH,
            preferred_element_type=jnp.float32).reshape(rows, ny, nz)
    for c in direct[1] + passed:
        c.wait_recv()
    edge = Halo(kap.at[0], kap.at[1], kap.at[deep], kap.at[deep + 1])
    edge.start()

    y_at = lax.broadcasted_iota(jnp.int32, (ny, nz), 0)
    z_at = lax.broadcasted_iota(jnp.int32, (ny, nz), 1)

    def faces(l, _):
        k = kap[l + 1]
        total = dlt[l]
        for ref, axis, shift, size, index, bound in (
            (cym, 0, 1, ny, y_at, 0), (cyp, 0, ny - 1, ny, y_at, ny - 1),
            (czm, 1, 1, nz, z_at, 0), (czp, 1, nz - 1, nz, z_at, nz - 1),
        ):
            near = pltpu.roll(k, shift, axis)
            f = 0.5 * (k + jnp.where(index == bound, 0.0, near))
            ref[l] = jnp.where(index == bound, 0.0, f)
            total = total + f
        kd[l] = total
        return 0

    lax.fori_loop(0, deep, faces, 0)
    edge.wait_recv()

    def across(l, _):
        cx[l] = 0.5 * (kap[l] + kap[l + 1])
        return 0

    lax.fori_loop(0, deep + 1, across, 0)

    def invert(l, _):
        d = kd[l] + cx[l] + cx[l + 1]
        kd[l] = d
        pre[l] = 1.0 / (d * d + obs[l])
        return 0

    lax.fori_loop(0, deep, invert, 0)

    chunks = [pl.ds(r, CHUNK) for r in range(0, ny, CHUNK)]

    def fold(x):
        x = x[:, :128] + x[:, 128:]
        return jnp.sum(x.reshape(CHUNK // 8, 8, 128), axis=0)

    def apply_k(field, p, l, r):
        rs = pl.ds(r, CHUNK)
        v = field[p, l + 1, rs]
        ym = pltpu.roll(v, 1, 0) if r == 0 else field[p, l + 1, pl.ds(r - 1, CHUNK)]
        yp = (pltpu.roll(v, CHUNK - 1, 0) if r + CHUNK == ny
              else field[p, l + 1, pl.ds(r + 1, CHUNK)])
        total = kd[l, rs] * v
        total = total - cx[l, rs] * field[p, l, rs]
        total = total - cx[l + 1, rs] * field[p, l + 2, rs]
        total = total - cym[l, rs] * ym
        total = total - cyp[l, rs] * yp
        total = total - czm[l, rs] * pltpu.roll(v, 1, 1)
        total = total - czp[l, rs] * pltpu.roll(v, nz - 1, 1)
        return total

    none = jnp.zeros((8, 128), jnp.float32)

    def put(ref, at, value):
        ref[at:at + 1] = jnp.sum(value, axis=0, keepdims=True)

    u_halo, t_halo, w_halo = [], [], []

    def begin(p):
        for c in swaps[p]:
            c.wait_recv()
        own[4 + p].wait()

        def layer(l, total):
            for rs in chunks:
                b = bp[p, l, rs]
                u = pre[l, rs] * b
                uu[p, l + 1, rs] = u
                total = total + fold(b * u)
            return total

        put(part1, 2 * p, lax.fori_loop(0, deep, layer, none))
        h = halo_of(uu, p)
        h.start()
        u_halo.append(h)

    def first(p):
        u_halo[p].wait_recv()

        def layer(l, total):
            for r in range(0, ny, CHUNK):
                rs = pl.ds(r, CHUNK)
                t = apply_k(uu, p, l, r)
                tt[p, l + 1, rs] = t
                u = uu[p, l + 1, rs]
                total = total + fold(t * t + obs[l, rs] * u * u)
            return total

        put(part1, 2 * p + 1, lax.fori_loop(0, deep, layer, none))
        h = halo_of(tt, p)
        h.start()
        t_halo.append(h)

    def second(p):
        t_halo[p].wait_recv()

        def layer(l, _):
            for r in range(0, ny, CHUNK):
                rs = pl.ds(r, CHUNK)
                q = apply_k(tt, p, l, r) + obs[l, rs] * uu[p, l + 1, rs]
                qq[p, l, rs] = q
                ww[p, l + 1, rs] = pre[l, rs] * q
            return 0

        lax.fori_loop(0, deep, layer, 0)
        h = halo_of(ww, p)
        h.start()
        w_halo.append(h)

    def share_sum(part, slots):
        sent = [remote(part, slots.at[g], other) for other in column]
        for c in sent:
            c.start()
        slots[g] = part[...]
        return sent

    def total_of(sent, slots):
        for c in sent:
            c.wait_recv()
        total = slots[0]
        for k in range(1, ng):
            total = total + slots[k]
        return jnp.sum(total, axis=1, keepdims=True)

    for i in range(share + 2):
        if i < share:
            begin(i)
        if 1 <= i <= share:
            first(i - 1)
        if i == share:
            sent1 = share_sum(part1, sum1)
        if i >= 2:
            second(i - 2)
    sums = total_of(sent1, sum1)
    gamma = [sums[2 * p:2 * p + 1] for p in range(share)]
    curve = [sums[2 * p + 1:2 * p + 2] for p in range(share)]
    alpha = [gamma[p] / curve[p] for p in range(share)]
    for p in range(share):
        w_halo[p].wait_recv()
        a = alpha[p]

        def layer(l, totals):
            s_sum, e_sum, g_sum = totals
            for r in range(0, ny, CHUNK):
                rs = pl.ds(r, CHUNK)
                s = tt[p, l + 1, rs] - a * apply_k(ww, p, l, r)
                q = qq[p, l, rs]
                u = uu[p, l + 1, rs] - a * ww[p, l + 1, rs]
                resid = bp[p, l, rs] - a * q
                s_sum = s_sum + fold(s * s + obs[l, rs] * u * u)
                e_sum = e_sum + fold(u * q)
                g_sum = g_sum + fold(resid * u)
            return s_sum, e_sum, g_sum

        found = lax.fori_loop(0, deep, layer, (none, none, none))
        for k in range(3):
            put(part2, 4 * p + k, found[k])
        part2[4 * p + 3:4 * p + 4] = jnp.zeros((1, 128), jnp.float32)
    sent2 = share_sum(part2, sum2)
    sums = total_of(sent2, sum2)
    on_u, on_w = [], []
    for p in range(share):
        d2, e2, g2 = (sums[4 * p + k:4 * p + k + 1] for k in range(3))
        beta = g2 / gamma[p]
        step = g2 / (d2 + 2.0 * beta * e2 + beta * beta * curve[p])
        on_u.append(alpha[p] + step * (1.0 + beta))
        on_w.append(alpha[p] * step)

    def estimate(l, _):
        for rs in chunks:
            total = jnp.zeros((CHUNK, nz), jnp.float32)
            for p in range(share):
                x = on_u[p] * uu[p, l + 1, rs] - on_w[p] * ww[p, l + 1, rs]
                total = total + bp[p, l, rs] * x
            acc[l, rs] = total
        return 0

    lax.fori_loop(0, deep, estimate, 0)
    near = [remote(acc.at[pl.ds(rows * mates[3], rows)], red1.at[1], mate(1)),
            remote(acc.at[pl.ds(rows * mates[1], rows)], red1.at[0], mate(1))]
    for c in near:
        c.start()
    near[0].wait_recv()
    relay[...] = acc[pl.ds(rows * mates[2], rows)] + red1[1]
    across_y = remote(relay, red2, mate(2))
    across_y.start()
    near[1].wait_recv()
    partial = acc[pl.ds(rows * j, rows)] + red1[0]
    across_y.wait_recv()
    diag = (partial + red2[...]) * (0.5 / probes.shape[0])
    out[...] = diag

    local = cells[...] - me * (rows * ny * nz)
    row = lax.div(local, nz)
    col = local - row * nz
    sens = local.shape[1]
    at_row = lax.broadcasted_iota(jnp.int32, (rows * ny, sens), 0) == row
    at_col = lax.broadcasted_iota(jnp.int32, (nz, sens), 0) == col
    picked = lax.dot_general(
        diag.reshape(rows * ny, nz), jnp.where(at_col, 1.0, 0.0),
        (((1,), (0,)), ((), ())), precision=HIGH, preferred_element_type=jnp.float32)
    grad[...] = jnp.sum(jnp.where(at_row, picked, 0.0), axis=0, keepdims=True)

    for c in direct[1] + direct[2] + listed + passed + near + [across_y] + sent1 + sent2:
        c.wait_send()
    for group in swaps:
        for c in group:
            c.wait_send()
    for h in [edge] + u_halo + t_halo + w_halo:
        h.wait_send()
    assert counter[0] == sems


def shards(probes, kappa, delta, sensor_cells, sensor_weights):
    count, rows, ny, nz = probes.shape
    ng = lax.axis_size("gx") // GROUP
    share, deep = count // GROUP, GROUP * rows
    sens = sensor_cells.shape[0]
    sems = 4 + 6 + 3 * share + 2 + 2 + 6 * share + 2 * (ng - 1) + 3
    f32 = jnp.float32
    field = pltpu.VMEM((deep, ny, nz), f32)
    padded = pltpu.VMEM((share, deep + 2, ny, nz), f32)
    plain = pltpu.VMEM((share, deep, ny, nz), f32)
    any_ = pl.BlockSpec(memory_space=pl.ANY)
    vmem = pl.BlockSpec(memory_space=pltpu.VMEM)
    diag, grad = pl.pallas_call(
        functools.partial(body, ng, sems),
        out_shape=(jax.ShapeDtypeStruct((rows, ny, nz), f32),
                   jax.ShapeDtypeStruct((1, sens), f32)),
        in_specs=[any_, any_, any_, vmem, vmem],
        out_specs=(vmem, vmem),
        scratch_shapes=[
            plain, padded, padded, padded, plain,
            pltpu.VMEM((deep + 2, ny, nz), f32), field, field, field, field,
            pltpu.VMEM((deep + 1, ny, nz), f32), field, field, field, field,
            pltpu.VMEM((GROUP, 1, sens), jnp.int32),
            pltpu.VMEM((GROUP, 1, sens), f32),
            pltpu.VMEM((2 * share, 128), f32),
            pltpu.VMEM((4 * share, 128), f32),
            pltpu.VMEM((ng, 2 * share, 128), f32),
            pltpu.VMEM((ng, 4 * share, 128), f32),
            field,
            pltpu.VMEM((2, rows, ny, nz), f32),
            pltpu.VMEM((rows, ny, nz), f32),
            pltpu.VMEM((rows, ny, nz), f32),
            pltpu.SemaphoreType.DMA((sems,)),
            pltpu.SemaphoreType.DMA((sems,)),
            pltpu.SemaphoreType.DMA((4 + share,)),
        ],
        compiler_params=pltpu.CompilerParams(
            collective_id=0, has_side_effects=True,
            vmem_limit_bytes=52 * 1024 * 1024),
        cost_estimate=pl.CostEstimate(
            flops=100 * probes.size, bytes_accessed=6 * probes.size, transcendentals=0),
    )(probes, kappa, delta, sensor_cells.reshape(1, sens), sensor_weights.reshape(1, sens))
    return diag, grad.reshape(sens)


def solution(mesh):
    placed = (
        P("grp", "gx", None, None),
        P(("grp", "gx"), None, None),
        P(("grp", "gx"), None, None),
        P(("grp", "gx")),
        P(("grp", "gx")),
    )
    return jax.shard_map(
        shards,
        mesh=mesh,
        in_specs=placed,
        out_specs=(P(("grp", "gx"), None, None), P(("grp", "gx"))),
        check_vma=False,
    )
```

```python
import functools

import jax
import jax.numpy as jnp
from jax import lax
from jax.experimental import pallas as pl
from jax.experimental.pallas import tpu as pltpu
from jax.sharding import PartitionSpec as P

GROUP = 4
CHUNK = 32
HIGH = lax.Precision.HIGHEST


def body(ng, sems, probes, kappa, delta, cells, weights, out, grad,
         bp, uu, tt, ww, qq, kap, dlt, kd, pre, obs, cx, cym, cyp, czm, czp,
         sc, sw, part1, part2, sum1, sum2, acc, red1, red2, relay,
         send_sem, recv_sem, local_sem):
    share = probes.shape[0] // GROUP
    rows, ny, nz = kappa.shape
    deep = GROUP * rows
    me = lax.axis_index("gx")
    g = lax.div(me, GROUP)
    j = lax.rem(me, GROUP)
    mates = {1: j + 1 - 2 * lax.rem(j, 2), 2: lax.rem(j + 2, 4), 3: 3 - j}
    has_low = g > 0
    has_high = g < ng - 1
    counter = [0]

    def remote(src, dst, target):
        k = counter[0]
        counter[0] += 1
        return pltpu.make_async_remote_copy(
            src_ref=src, dst_ref=dst, send_sem=send_sem.at[k],
            recv_sem=recv_sem.at[k], device_id={"gx": target},
            device_id_type=pl.DeviceIdType.MESH)

    barrier = pltpu.get_barrier_semaphore()
    for k in mates:
        pl.semaphore_signal(barrier, inc=1, device_id={"gx": g * GROUP + mates[k]},
                            device_id_type=pl.DeviceIdType.MESH)
    column = [lax.rem(g + d, ng) * GROUP + j for d in range(1, ng)]
    for other in column:
        pl.semaphore_signal(barrier, inc=1, device_id={"gx": other},
                            device_id_type=pl.DeviceIdType.MESH)
    pl.semaphore_wait(barrier, 3 + ng - 1)

    def mate(k):
        return g * GROUP + mates[k]

    mine_k = kap.at[pl.ds(1 + rows * j, rows)]
    mine_d = dlt.at[pl.ds(rows * j, rows)]
    direct = {}
    for k in (2, 1):
        direct[k] = [remote(kappa, mine_k, mate(k)), remote(delta, mine_d, mate(k))]
        for c in direct[k]:
            c.start()
    listed = []
    for k in (2, 3, 1):
        listed += [remote(cells, sc.at[j], mate(k)), remote(weights, sw.at[j], mate(k))]
    for c in listed:
        c.start()
    swaps = []
    edge_row = lax.div(j, 2)
    for row in (edge_row, 1 - edge_row):
        for p in range(share):
            group = []
            for k in (2, 3, 1):
                c = remote(probes.at[share * mates[k] + p, pl.ds(row, 1)],
                           bp.at[p, pl.ds(rows * j + row, 1)], mate(k))
                c.start()
                group.append(c)
            swaps.append(group)
    own = [
        pltpu.make_async_copy(kappa, mine_k, local_sem.at[0]),
        pltpu.make_async_copy(delta, mine_d, local_sem.at[1]),
        pltpu.make_async_copy(cells, sc.at[j], local_sem.at[2]),
        pltpu.make_async_copy(weights, sw.at[j], local_sem.at[3]),
    ] + [
        pltpu.make_async_copy(probes.at[share * j + p],
                              bp.at[p, pl.ds(rows * j, rows)], local_sem.at[4 + p])
        for p in range(share)
    ]
    for c in own:
        c.start()

    class Halo:
        def __init__(self, low, first, last, high):
            self.up = remote(last, low, me + GROUP)
            self.down = remote(first, high, me - GROUP)

        def start(self):
            pl.when(has_high)(self.up.start)
            pl.when(has_low)(self.down.start)

        def wait_recv(self):
            pl.when(has_low)(self.up.wait_recv)
            pl.when(has_high)(self.down.wait_recv)

        def wait_send(self):
            pl.when(has_high)(self.up.wait_send)
            pl.when(has_low)(self.down.wait_send)

    def halo_of(field, p):
        f = field.at[p]
        return Halo(f.at[0], f.at[1], f.at[deep], f.at[deep + 1])

    zero = jnp.zeros((ny, nz), jnp.float32)

    @pl.when(g == 0)
    def _():
        kap[0] = zero
        for p in range(share):
            uu[p, 0] = zero
            tt[p, 0] = zero
            ww[p, 0] = zero

    @pl.when(g == ng - 1)
    def _():
        kap[deep + 1] = zero
        for p in range(share):
            uu[p, deep + 1] = zero
            tt[p, deep + 1] = zero
            ww[p, deep + 1] = zero

    for c in direct[2]:
        c.wait_recv()
    far_k = kap.at[pl.ds(1 + rows * mates[2], rows)]
    far_d = dlt.at[pl.ds(rows * mates[2], rows)]
    passed = [remote(far_k, far_k, mate(1)), remote(far_d, far_d, mate(1))]
    for c in passed:
        c.start()
    for c in listed:
        c.wait_recv()
    for c in own[:4]:
        c.wait()
    for k in range(GROUP):
        local = sc[k] - (g * GROUP + k) * (rows * ny * nz)
        row = lax.div(local, nz)
        col = local - row * nz
        sens = local.shape[1]
        at_row = lax.broadcasted_iota(jnp.int32, (rows * ny, sens), 0) == row
        at_col = lax.broadcasted_iota(jnp.int32, (nz, sens), 0) == col
        left = jnp.where(at_row, sw[k], 0.0)
        right = jnp.where(at_col, 1.0, 0.0)
        obs[rows * k:rows * (k + 1)] = lax.dot_general(
            left, right, (((1,), (1,)), ((), ())), precision=HIGH,
            preferred_element_type=jnp.float32).reshape(rows, ny, nz)
    for c in direct[1] + passed:
        c.wait_recv()
    edge = Halo(kap.at[0], kap.at[1], kap.at[deep], kap.at[deep + 1])
    edge.start()

    y_at = lax.broadcasted_iota(jnp.int32, (ny, nz), 0)
    z_at = lax.broadcasted_iota(jnp.int32, (ny, nz), 1)

    def faces(l, _):
        k = kap[l + 1]
        total = dlt[l]
        for ref, axis, shift, size, index, bound in (
            (cym, 0, 1, ny, y_at, 0), (cyp, 0, ny - 1, ny, y_at, ny - 1),
            (czm, 1, 1, nz, z_at, 0), (czp, 1, nz - 1, nz, z_at, nz - 1),
        ):
            near = pltpu.roll(k, shift, axis)
            f = 0.5 * (k + jnp.where(index == bound, 0.0, near))
            ref[l] = jnp.where(index == bound, 0.0, f)
            total = total + f
        kd[l] = total
        return 0

    lax.fori_loop(0, deep, faces, 0)
    edge.wait_recv()

    def across(l, _):
        cx[l] = 0.5 * (kap[l] + kap[l + 1])
        return 0

    lax.fori_loop(0, deep + 1, across, 0)

    def invert(l, _):
        d = kd[l] + cx[l] + cx[l + 1]
        kd[l] = d
        pre[l] = 1.0 / (d * d + obs[l])
        return 0

    lax.fori_loop(0, deep, invert, 0)

    chunks = [pl.ds(r, CHUNK) for r in range(0, ny, CHUNK)]

    def fold(x):
        x = x[:, :128] + x[:, 128:]
        return jnp.sum(x.reshape(CHUNK // 8, 8, 128), axis=0)

    def apply_k(field, p, l, r):
        rs = pl.ds(r, CHUNK)
        v = field[p, l + 1, rs]
        ym = pltpu.roll(v, 1, 0) if r == 0 else field[p, l + 1, pl.ds(r - 1, CHUNK)]
        yp = (pltpu.roll(v, CHUNK - 1, 0) if r + CHUNK == ny
              else field[p, l + 1, pl.ds(r + 1, CHUNK)])
        total = kd[l, rs] * v
        total = total - cx[l, rs] * field[p, l, rs]
        total = total - cx[l + 1, rs] * field[p, l + 2, rs]
        total = total - cym[l, rs] * ym
        total = total - cyp[l, rs] * yp
        total = total - czm[l, rs] * pltpu.roll(v, 1, 1)
        total = total - czp[l, rs] * pltpu.roll(v, nz - 1, 1)
        return total

    none = jnp.zeros((8, 128), jnp.float32)

    def put(ref, at, value):
        ref[at:at + 1] = jnp.sum(value, axis=0, keepdims=True)

    u_halo, t_halo, w_halo, sent1 = [], [], [], []

    def border(p):
        for c in swaps[p]:
            c.wait_recv()
        own[4 + p].wait()
        uu[p, 1] = pre[0] * bp[p, 0]
        uu[p, deep] = pre[deep - 1] * bp[p, deep - 1]
        h = halo_of(uu, p)
        h.start()
        u_halo.append(h)

    def first(p):
        for c in swaps[share + p]:
            c.wait_recv()

        def scale(l, _):
            uu[p, l + 1] = pre[l] * bp[p, l]
            return 0

        lax.fori_loop(1, deep - 1, scale, 0)
        u_halo[p].wait_recv()

        def layer(l, totals):
            g_sum, c_sum = totals
            for r in range(0, ny, CHUNK):
                rs = pl.ds(r, CHUNK)
                t = apply_k(uu, p, l, r)
                tt[p, l + 1, rs] = t
                u = uu[p, l + 1, rs]
                g_sum = g_sum + fold(bp[p, l, rs] * u)
                c_sum = c_sum + fold(t * t + obs[l, rs] * u * u)
            return g_sum, c_sum

        found = lax.fori_loop(0, deep, layer, (none, none))
        for k in range(2):
            put(part1.at[p], k, found[k])
        sent1.append(share_sum(part1.at[p], sum1.at[p]))
        h = halo_of(tt, p)
        h.start()
        t_halo.append(h)

    def second(p):
        t_halo[p].wait_recv()

        def layer(l, _):
            for r in range(0, ny, CHUNK):
                rs = pl.ds(r, CHUNK)
                q = apply_k(tt, p, l, r) + obs[l, rs] * uu[p, l + 1, rs]
                qq[p, l, rs] = q
                ww[p, l + 1, rs] = pre[l, rs] * q
            return 0

        lax.fori_loop(0, deep, layer, 0)
        h = halo_of(ww, p)
        h.start()
        w_halo.append(h)

    def share_sum(part, slots):
        sent = [remote(part, slots.at[g], other) for other in column]
        for c in sent:
            c.start()
        slots[g] = part[...]
        return sent

    def total_of(sent, slots):
        for c in sent:
            c.wait_recv()
        total = slots[0]
        for k in range(1, ng):
            total = total + slots[k]
        return jnp.sum(total, axis=1, keepdims=True)

    gamma, curve, alpha = [], [], []

    def third(p):
        sums = total_of(sent1[p], sum1.at[p])
        gamma.append(sums[0:1])
        curve.append(sums[1:2])
        a = gamma[p] / curve[p]
        alpha.append(a)
        w_halo[p].wait_recv()

        def layer(l, totals):
            s_sum, e_sum, g_sum = totals
            for r in range(0, ny, CHUNK):
                rs = pl.ds(r, CHUNK)
                s = tt[p, l + 1, rs] - a * apply_k(ww, p, l, r)
                q = qq[p, l, rs]
                u = uu[p, l + 1, rs] - a * ww[p, l + 1, rs]
                resid = bp[p, l, rs] - a * q
                s_sum = s_sum + fold(s * s + obs[l, rs] * u * u)
                e_sum = e_sum + fold(u * q)
                g_sum = g_sum + fold(resid * u)
            return s_sum, e_sum, g_sum

        found = lax.fori_loop(0, deep, layer, (none, none, none))
        for k in range(3):
            put(part2, 4 * p + k, found[k])
        part2[4 * p + 3:4 * p + 4] = jnp.zeros((1, 128), jnp.float32)

    for p in range(share):
        border(p)
    for i in range(share):
        first(i)
        if 1 <= i:
            second(i - 1)
        if 2 <= i:
            third(i - 2)
    second(share - 1)
    third(share - 2)
    third(share - 1)
    sent2 = share_sum(part2, sum2)
    sums = total_of(sent2, sum2)
    on_u, on_w = [], []
    for p in range(share):
        d2, e2, g2 = (sums[4 * p + k:4 * p + k + 1] for k in range(3))
        beta = g2 / gamma[p]
        step = g2 / (d2 + 2.0 * beta * e2 + beta * beta * curve[p])
        on_u.append(alpha[p] + step * (1.0 + beta))
        on_w.append(alpha[p] * step)

    def estimate(l, _):
        for rs in chunks:
            total = jnp.zeros((CHUNK, nz), jnp.float32)
            for p in range(share):
                x = on_u[p] * uu[p, l + 1, rs] - on_w[p] * ww[p, l + 1, rs]
                total = total + bp[p, l, rs] * x
            acc[l, rs] = total
        return 0

    def block(at):
        lax.fori_loop(rows * at, rows * at + rows, estimate, 0)

    block(mates[3])
    near = [remote(acc.at[pl.ds(rows * mates[3], rows)], red1.at[1], mate(1)),
            remote(acc.at[pl.ds(rows * mates[1], rows)], red1.at[0], mate(1))]
    near[0].start()
    block(mates[2])
    near[0].wait_recv()
    relay[...] = acc[pl.ds(rows * mates[2], rows)] + red1[1]
    across_y = remote(relay, red2, mate(2))
    across_y.start()
    block(mates[1])
    near[1].start()
    block(j)
    near[1].wait_recv()
    partial = acc[pl.ds(rows * j, rows)] + red1[0]
    across_y.wait_recv()
    diag = (partial + red2[...]) * (0.5 / probes.shape[0])
    out[...] = diag

    local = sc[j] - me * (rows * ny * nz)
    row = lax.div(local, nz)
    col = local - row * nz
    sens = local.shape[1]
    at_row = lax.broadcasted_iota(jnp.int32, (rows * ny, sens), 0) == row
    at_col = lax.broadcasted_iota(jnp.int32, (nz, sens), 0) == col
    picked = lax.dot_general(
        diag.reshape(rows * ny, nz), jnp.where(at_col, 1.0, 0.0),
        (((1,), (0,)), ((), ())), precision=HIGH, preferred_element_type=jnp.float32)
    grad[...] = jnp.sum(jnp.where(at_row, picked, 0.0), axis=0, keepdims=True)

    for c in direct[1] + direct[2] + listed + passed + near + [across_y] + sum(sent1, sent2):
        c.wait_send()
    for group in swaps:
        for c in group:
            c.wait_send()
    for h in [edge] + u_halo + t_halo + w_halo:
        h.wait_send()
    assert counter[0] == sems


def shards(probes, kappa, delta, sensor_cells, sensor_weights):
    count, rows, ny, nz = probes.shape
    ng = lax.axis_size("gx") // GROUP
    share, deep = count // GROUP, GROUP * rows
    sens = sensor_cells.shape[0]
    sems = 4 + 6 + 6 * share + 2 + 2 + 6 * share + (share + 1) * (ng - 1) + 3
    f32 = jnp.float32
    field = pltpu.VMEM((deep, ny, nz), f32)
    padded = pltpu.VMEM((share, deep + 2, ny, nz), f32)
    plain = pltpu.VMEM((share, deep, ny, nz), f32)
    any_ = pl.BlockSpec(memory_space=pl.ANY)
    vmem = pl.BlockSpec(memory_space=pltpu.VMEM)
    diag, grad = pl.pallas_call(
        functools.partial(body, ng, sems),
        out_shape=(jax.ShapeDtypeStruct((rows, ny, nz), f32),
                   jax.ShapeDtypeStruct((1, sens), f32)),
        in_specs=[any_] * 5,
        out_specs=(vmem, vmem),
        scratch_shapes=[
            plain, padded, padded, padded, plain,
            pltpu.VMEM((deep + 2, ny, nz), f32), field, field, field, field,
            pltpu.VMEM((deep + 1, ny, nz), f32), field, field, field, field,
            pltpu.VMEM((GROUP, 1, sens), jnp.int32),
            pltpu.VMEM((GROUP, 1, sens), f32),
            pltpu.VMEM((share, 2, 128), f32),
            pltpu.VMEM((4 * share, 128), f32),
            pltpu.VMEM((share, ng, 2, 128), f32),
            pltpu.VMEM((ng, 4 * share, 128), f32),
            field,
            pltpu.VMEM((2, rows, ny, nz), f32),
            pltpu.VMEM((rows, ny, nz), f32),
            pltpu.VMEM((rows, ny, nz), f32),
            pltpu.SemaphoreType.DMA((sems,)),
            pltpu.SemaphoreType.DMA((sems,)),
            pltpu.SemaphoreType.DMA((4 + share,)),
        ],
        compiler_params=pltpu.CompilerParams(
            collective_id=0, has_side_effects=True,
            vmem_limit_bytes=60 * 1024 * 1024),
        cost_estimate=pl.CostEstimate(
            flops=100 * probes.size, bytes_accessed=6 * probes.size, transcendentals=0),
    )(probes, kappa, delta, sensor_cells.reshape(1, sens), sensor_weights.reshape(1, sens))
    return diag, grad.reshape(sens)


def solution(mesh):
    placed = (
        P("grp", "gx", None, None),
        P(("grp", "gx"), None, None),
        P(("grp", "gx"), None, None),
        P(("grp", "gx")),
        P(("grp", "gx")),
    )
    return jax.shard_map(
        shards,
        mesh=mesh,
        in_specs=placed,
        out_specs=(P(("grp", "gx"), None, None), P(("grp", "gx"))),
        check_vma=False,
    )
```

```python
import functools

import jax
import jax.numpy as jnp
from jax import lax
from jax.experimental import pallas as pl
from jax.experimental.pallas import tpu as pltpu
from jax.sharding import PartitionSpec as P

GROUP = 4
CHUNK = 32
HIGH = lax.Precision.HIGHEST


def body(ng, sems, probes, kappa, delta, cells, weights, out, grad,
         bp, uu, tt, ww, qq, kap, dlt, kd, pre, obs, cx, cym, cyp, czm, czp,
         sc, sw, part1, part2, sum1, sum2, acc, red1, red2, relay,
         send_sem, recv_sem, local_sem):
    share = probes.shape[0] // GROUP
    rows, ny, nz = kappa.shape
    deep = GROUP * rows
    me = lax.axis_index("gx")
    g = lax.div(me, GROUP)
    j = lax.rem(me, GROUP)
    mates = {1: j + 1 - 2 * lax.rem(j, 2), 2: lax.rem(j + 2, 4), 3: 3 - j}
    has_low = g > 0
    has_high = g < ng - 1
    counter = [0]

    def remote(src, dst, target):
        k = counter[0]
        counter[0] += 1
        return pltpu.make_async_remote_copy(
            src_ref=src, dst_ref=dst, send_sem=send_sem.at[k],
            recv_sem=recv_sem.at[k], device_id={"gx": target},
            device_id_type=pl.DeviceIdType.MESH)

    barrier = pltpu.get_barrier_semaphore()
    for k in mates:
        pl.semaphore_signal(barrier, inc=1, device_id={"gx": g * GROUP + mates[k]},
                            device_id_type=pl.DeviceIdType.MESH)
    column = [lax.rem(g + d, ng) * GROUP + j for d in range(1, ng)]
    for other in column:
        pl.semaphore_signal(barrier, inc=1, device_id={"gx": other},
                            device_id_type=pl.DeviceIdType.MESH)
    pl.semaphore_wait(barrier, 3 + ng - 1)

    def mate(k):
        return g * GROUP + mates[k]

    mine_k = kap.at[pl.ds(1 + rows * j, rows)]
    mine_d = dlt.at[pl.ds(rows * j, rows)]
    direct = {}
    for k in (2, 1):
        direct[k] = [remote(kappa, mine_k, mate(k)), remote(delta, mine_d, mate(k))]
        for c in direct[k]:
            c.start()
    listed = []
    for k in (2, 3, 1):
        listed += [remote(cells, sc.at[j], mate(k)), remote(weights, sw.at[j], mate(k))]
    for c in listed:
        c.start()
    swaps = []
    edge_row = lax.div(j, 2)
    for row in (edge_row, 1 - edge_row):
        for p in range(share):
            group = []
            for k in (2, 3, 1):
                c = remote(probes.at[share * mates[k] + p, pl.ds(row, 1)],
                           bp.at[p, pl.ds(rows * j + row, 1)], mate(k))
                c.start()
                group.append(c)
            swaps.append(group)
    own = [
        pltpu.make_async_copy(kappa, mine_k, local_sem.at[0]),
        pltpu.make_async_copy(delta, mine_d, local_sem.at[1]),
        pltpu.make_async_copy(cells, sc.at[j], local_sem.at[2]),
        pltpu.make_async_copy(weights, sw.at[j], local_sem.at[3]),
    ] + [
        pltpu.make_async_copy(probes.at[share * j + p],
                              bp.at[p, pl.ds(rows * j, rows)], local_sem.at[4 + p])
        for p in range(share)
    ]
    for c in own:
        c.start()

    class Halo:
        def __init__(self, low, first, last, high):
            self.up = remote(last, low, me + GROUP)
            self.down = remote(first, high, me - GROUP)

        def start(self):
            pl.when(has_high)(self.up.start)
            pl.when(has_low)(self.down.start)

        def wait_recv(self):
            pl.when(has_low)(self.up.wait_recv)
            pl.when(has_high)(self.down.wait_recv)

        def wait_send(self):
            pl.when(has_high)(self.up.wait_send)
            pl.when(has_low)(self.down.wait_send)

    def halo_of(field, p):
        f = field.at[p]
        return Halo(f.at[0], f.at[1], f.at[deep], f.at[deep + 1])

    zero = jnp.zeros((ny, nz), jnp.float32)

    @pl.when(g == 0)
    def _():
        kap[0] = zero
        for p in range(share):
            uu[p, 0] = zero
            tt[p, 0] = zero
            ww[p, 0] = zero

    @pl.when(g == ng - 1)
    def _():
        kap[deep + 1] = zero
        for p in range(share):
            uu[p, deep + 1] = zero
            tt[p, deep + 1] = zero
            ww[p, deep + 1] = zero

    for c in direct[2]:
        c.wait_recv()
    far_k = kap.at[pl.ds(1 + rows * mates[2], rows)]
    far_d = dlt.at[pl.ds(rows * mates[2], rows)]
    passed = [remote(far_k, far_k, mate(1)), remote(far_d, far_d, mate(1))]
    for c in passed:
        c.start()
    for c in listed:
        c.wait_recv()
    for c in own[:4]:
        c.wait()
    for k in range(GROUP):
        local = sc[k] - (g * GROUP + k) * (rows * ny * nz)
        row = lax.div(local, nz)
        col = local - row * nz
        sens = local.shape[1]
        at_row = lax.broadcasted_iota(jnp.int32, (rows * ny, sens), 0) == row
        at_col = lax.broadcasted_iota(jnp.int32, (nz, sens), 0) == col
        left = jnp.where(at_row, sw[k], 0.0)
        right = jnp.where(at_col, 1.0, 0.0)
        obs[rows * k:rows * (k + 1)] = lax.dot_general(
            left, right, (((1,), (1,)), ((), ())), precision=HIGH,
            preferred_element_type=jnp.float32).reshape(rows, ny, nz)
    for c in direct[1] + passed:
        c.wait_recv()
    edge = Halo(kap.at[0], kap.at[1], kap.at[deep], kap.at[deep + 1])
    edge.start()

    y_at = lax.broadcasted_iota(jnp.int32, (ny, nz), 0)
    z_at = lax.broadcasted_iota(jnp.int32, (ny, nz), 1)

    def faces(l, _):
        k = kap[l + 1]
        total = dlt[l]
        for ref, axis, shift, size, index, bound in (
            (cym, 0, 1, ny, y_at, 0), (cyp, 0, ny - 1, ny, y_at, ny - 1),
            (czm, 1, 1, nz, z_at, 0), (czp, 1, nz - 1, nz, z_at, nz - 1),
        ):
            near = pltpu.roll(k, shift, axis)
            f = 0.5 * (k + jnp.where(index == bound, 0.0, near))
            ref[l] = jnp.where(index == bound, 0.0, f)
            total = total + f
        kd[l] = total
        return 0

    lax.fori_loop(0, deep, faces, 0)
    edge.wait_recv()

    def across(l, _):
        cx[l] = 0.5 * (kap[l] + kap[l + 1])
        return 0

    lax.fori_loop(0, deep + 1, across, 0)

    def invert(l, _):
        d = kd[l] + cx[l] + cx[l + 1]
        kd[l] = d
        pre[l] = 1.0 / (d * d + obs[l])
        return 0

    lax.fori_loop(0, deep, invert, 0)

    chunks = [pl.ds(r, CHUNK) for r in range(0, ny, CHUNK)]

    def fold(x):
        x = x[:, :128] + x[:, 128:]
        return jnp.sum(x.reshape(CHUNK // 8, 8, 128), axis=0)

    def apply_k(field, p, l, r):
        rs = pl.ds(r, CHUNK)
        v = field[p, l + 1, rs]
        ym = pltpu.roll(v, 1, 0) if r == 0 else field[p, l + 1, pl.ds(r - 1, CHUNK)]
        yp = (pltpu.roll(v, CHUNK - 1, 0) if r + CHUNK == ny
              else field[p, l + 1, pl.ds(r + 1, CHUNK)])
        total = kd[l, rs] * v
        total = total - cx[l, rs] * field[p, l, rs]
        total = total - cx[l + 1, rs] * field[p, l + 2, rs]
        total = total - cym[l, rs] * ym
        total = total - cyp[l, rs] * yp
        total = total - czm[l, rs] * pltpu.roll(v, 1, 1)
        total = total - czp[l, rs] * pltpu.roll(v, nz - 1, 1)
        return total

    none = jnp.zeros((8, 128), jnp.float32)

    def put(ref, at, value):
        ref[at:at + 1] = jnp.sum(value, axis=0, keepdims=True)

    u_halo, t_halo, w_halo, sent1 = [], [], [], []

    def border(p):
        for c in swaps[p]:
            c.wait_recv()
        own[4 + p].wait()
        uu[p, 1] = pre[0] * bp[p, 0]
        uu[p, deep] = pre[deep - 1] * bp[p, deep - 1]
        h = halo_of(uu, p)
        h.start()
        u_halo.append(h)

    def first(p):
        for c in swaps[share + p]:
            c.wait_recv()

        def scale(l, _):
            uu[p, l + 1] = pre[l] * bp[p, l]
            return 0

        lax.fori_loop(1, deep - 1, scale, 0)
        u_halo[p].wait_recv()

        def layer(l, totals):
            g_sum, c_sum = totals
            for r in range(0, ny, CHUNK):
                rs = pl.ds(r, CHUNK)
                t = apply_k(uu, p, l, r)
                tt[p, l + 1, rs] = t
                u = uu[p, l + 1, rs]
                g_sum = g_sum + fold(bp[p, l, rs] * u)
                c_sum = c_sum + fold(t * t + obs[l, rs] * u * u)
            return g_sum, c_sum

        found = layer(deep - 1, layer(0, (none, none)))
        h = halo_of(tt, p)
        h.start()
        t_halo.append(h)
        found = lax.fori_loop(1, deep - 1, layer, found)
        for k in range(2):
            put(part1.at[p], k, found[k])
        sent1.append(share_sum(part1.at[p], sum1.at[p]))

    def second(p):
        def layer(l, _):
            for r in range(0, ny, CHUNK):
                rs = pl.ds(r, CHUNK)
                q = apply_k(tt, p, l, r) + obs[l, rs] * uu[p, l + 1, rs]
                qq[p, l, rs] = q
                ww[p, l + 1, rs] = pre[l, rs] * q
            return 0

        lax.fori_loop(1, deep - 1, layer, 0)
        t_halo[p].wait_recv()
        layer(0, 0)
        layer(deep - 1, 0)
        h = halo_of(ww, p)
        h.start()
        w_halo.append(h)

    def share_sum(part, slots):
        sent = [remote(part, slots.at[g], other) for other in column]
        for c in sent:
            c.start()
        slots[g] = part[...]
        return sent

    def total_of(sent, slots):
        for c in sent:
            c.wait_recv()
        total = slots[0]
        for k in range(1, ng):
            total = total + slots[k]
        return jnp.sum(total, axis=1, keepdims=True)

    gamma, curve, alpha = [], [], []

    def third(p):
        sums = total_of(sent1[p], sum1.at[p])
        gamma.append(sums[0:1])
        curve.append(sums[1:2])
        a = gamma[p] / curve[p]
        alpha.append(a)

        def layer(l, totals):
            s_sum, e_sum, g_sum = totals
            for r in range(0, ny, CHUNK):
                rs = pl.ds(r, CHUNK)
                s = tt[p, l + 1, rs] - a * apply_k(ww, p, l, r)
                q = qq[p, l, rs]
                u = uu[p, l + 1, rs] - a * ww[p, l + 1, rs]
                resid = bp[p, l, rs] - a * q
                s_sum = s_sum + fold(s * s + obs[l, rs] * u * u)
                e_sum = e_sum + fold(u * q)
                g_sum = g_sum + fold(resid * u)
            return s_sum, e_sum, g_sum

        found = lax.fori_loop(1, deep - 1, layer, (none, none, none))
        w_halo[p].wait_recv()
        found = layer(deep - 1, layer(0, found))
        for k in range(3):
            put(part2, 4 * p + k, found[k])
        part2[4 * p + 3:4 * p + 4] = jnp.zeros((1, 128), jnp.float32)

    for p in range(share):
        border(p)
    for i in range(share):
        first(i)
        if 1 <= i:
            second(i - 1)
        if 2 <= i:
            third(i - 2)
    second(share - 1)
    third(share - 2)
    third(share - 1)
    sent2 = share_sum(part2, sum2)
    sums = total_of(sent2, sum2)
    on_u, on_w = [], []
    for p in range(share):
        d2, e2, g2 = (sums[4 * p + k:4 * p + k + 1] for k in range(3))
        beta = g2 / gamma[p]
        step = g2 / (d2 + 2.0 * beta * e2 + beta * beta * curve[p])
        on_u.append(alpha[p] + step * (1.0 + beta))
        on_w.append(alpha[p] * step)

    def estimate(l, _):
        for rs in chunks:
            total = jnp.zeros((CHUNK, nz), jnp.float32)
            for p in range(share):
                x = on_u[p] * uu[p, l + 1, rs] - on_w[p] * ww[p, l + 1, rs]
                total = total + bp[p, l, rs] * x
            acc[l, rs] = total
        return 0

    def slab(at):
        return [rows * at + i for i in range(rows)]

    def one(ref, at):
        return ref.at[pl.ds(at, 1)]

    far, near, across_y = [], [], []
    for i, at in enumerate(slab(mates[3])):
        estimate(at, 0)
        c = remote(one(acc, at), one(red1.at[1], i), mate(1))
        c.start()
        far.append(c)
    for i, at in enumerate(slab(mates[2])):
        estimate(at, 0)
        far[i].wait_recv()
        relay[i] = acc[at] + red1[1, i]
        c = remote(one(relay, i), one(red2, i), mate(2))
        c.start()
        across_y.append(c)
    for i, at in enumerate(slab(mates[1])):
        estimate(at, 0)
        c = remote(one(acc, at), one(red1.at[0], i), mate(1))
        c.start()
        near.append(c)
    for at in slab(j):
        estimate(at, 0)

    local = sc[j] - me * (rows * ny * nz)
    row = lax.div(local, nz)
    col = local - row * nz
    sens = local.shape[1]
    y_row = lax.broadcasted_iota(jnp.int32, (ny, sens), 0)
    at_col = lax.broadcasted_iota(jnp.int32, (nz, sens), 0) == col
    hot = jnp.where(at_col, 1.0, 0.0)
    for i, at in enumerate(slab(j)):
        near[i].wait_recv()
        partial = acc[at] + red1[0, i]
        across_y[i].wait_recv()
        diag = (partial + red2[i]) * (0.5 / probes.shape[0])
        out[i] = diag
        picked = lax.dot_general(
            diag, hot, (((1,), (0,)), ((), ())), precision=HIGH,
            preferred_element_type=jnp.float32)
        found = jnp.sum(jnp.where(y_row + i * ny == row, picked, 0.0),
                        axis=0, keepdims=True)
        grad[...] = found if i == 0 else grad[...] + found

    for c in direct[1] + direct[2] + listed + passed + far + near + across_y + sum(sent1, sent2):
        c.wait_send()
    for group in swaps:
        for c in group:
            c.wait_send()
    for h in [edge] + u_halo + t_halo + w_halo:
        h.wait_send()
    assert counter[0] == sems


def shards(probes, kappa, delta, sensor_cells, sensor_weights):
    count, rows, ny, nz = probes.shape
    ng = lax.axis_size("gx") // GROUP
    share, deep = count // GROUP, GROUP * rows
    sens = sensor_cells.shape[0]
    sems = 4 + 6 + 6 * share + 2 + 2 + 6 * share + (share + 1) * (ng - 1) + 3 * rows
    f32 = jnp.float32
    field = pltpu.VMEM((deep, ny, nz), f32)
    padded = pltpu.VMEM((share, deep + 2, ny, nz), f32)
    plain = pltpu.VMEM((share, deep, ny, nz), f32)
    any_ = pl.BlockSpec(memory_space=pl.ANY)
    vmem = pl.BlockSpec(memory_space=pltpu.VMEM)
    diag, grad = pl.pallas_call(
        functools.partial(body, ng, sems),
        out_shape=(jax.ShapeDtypeStruct((rows, ny, nz), f32),
                   jax.ShapeDtypeStruct((1, sens), f32)),
        in_specs=[any_] * 5,
        out_specs=(vmem, vmem),
        scratch_shapes=[
            plain, padded, padded, padded, plain,
            pltpu.VMEM((deep + 2, ny, nz), f32), field, field, field, field,
            pltpu.VMEM((deep + 1, ny, nz), f32), field, field, field, field,
            pltpu.VMEM((GROUP, 1, sens), jnp.int32),
            pltpu.VMEM((GROUP, 1, sens), f32),
            pltpu.VMEM((share, 2, 128), f32),
            pltpu.VMEM((4 * share, 128), f32),
            pltpu.VMEM((share, ng, 2, 128), f32),
            pltpu.VMEM((ng, 4 * share, 128), f32),
            field,
            pltpu.VMEM((2, rows, ny, nz), f32),
            pltpu.VMEM((rows, ny, nz), f32),
            pltpu.VMEM((rows, ny, nz), f32),
            pltpu.SemaphoreType.DMA((sems,)),
            pltpu.SemaphoreType.DMA((sems,)),
            pltpu.SemaphoreType.DMA((4 + share,)),
        ],
        compiler_params=pltpu.CompilerParams(
            collective_id=0, has_side_effects=True,
            vmem_limit_bytes=60 * 1024 * 1024),
        cost_estimate=pl.CostEstimate(
            flops=100 * probes.size, bytes_accessed=6 * probes.size, transcendentals=0),
    )(probes, kappa, delta, sensor_cells.reshape(1, sens), sensor_weights.reshape(1, sens))
    return diag, grad.reshape(sens)


def solution(mesh):
    placed = (
        P("grp", "gx", None, None),
        P(("grp", "gx"), None, None),
        P(("grp", "gx"), None, None),
        P(("grp", "gx")),
        P(("grp", "gx")),
    )
    return jax.shard_map(
        shards,
        mesh=mesh,
        in_specs=placed,
        out_specs=(P(("grp", "gx"), None, None), P(("grp", "gx"))),
        check_vma=False,
    )
```
